512 devices in a mesh: grp: 16 (over y, x), ep: 32 (over z, core).
Axes of the slice: x: 4, y: 4, z: 16, core: 2. Of those that a mesh axis runs over, the one named last changes fastest.
Arguments:
- tokens: bfloat16 [4096, 4096], P(('grp', 'ep')), may hold values from -6 to 6
- expert_ids: int32 [4096, 8], P(('grp', 'ep')), may hold values from 0 to 63, all different within a row; in each aligned block of 8 rows (0 to 7, 8 to 15, ...) at most 2 rows name the same one
- gate_weights: float32 [4096, 8], P(('grp', 'ep')), may hold values from 0.1 to 1
- w_gate: bfloat16 [32, 4096, 2048], P('ep', None, 'grp'), may hold values from -0.09375 to 0.09375
- w_up: bfloat16 [32, 4096, 2048], P('ep', None, 'grp'), may hold values from -0.09375 to 0.09375
- w_down: bfloat16 [32, 1024, 8192], P('ep', None, 'grp'), may hold values from -0.1875 to 0.1875
- norm_gain: float32 [4096], replicated, may hold values from 0.1 to 1.9
Outputs:
- scored: bfloat16 [4096, 4096], P(('grp', 'ep'))
The draws below stay inside these ranges and needn't reach their ends.
Inputs may be any that keep to these rules, and one draw needn't show every extreme that they name: `expert_ids`: each row names 8 different experts. Among the 8 rows of one device no expert is named by more than 2 rows, and in some devices' rows an expert is named by exactly 2.
All inputs are finite; a program needn't handle non-finite values.
Results may differ from the reference program's by a relative error of at most 0.0043.
Values may be sent and summed in bfloat16 or wider, within the bound.
No kernel may reach another device: no remote copies, remote signals or barrier semaphores. Data moves between devices by JAX's collectives and lax.ppermute only.
A program may use at most 64 MiB of HBM per device.

```python
import math
import jax
import jax.numpy as jnp
import numpy as np
from jax import lax

D = 4096
TOP = 8
FF = 1024
TOK_DEV = 8
EXPERTS = 64
CAP = 2
TOKENS = 4096
N_GRP = 16
N_EP = 32


def levels(stream_key, extent, pieces, low, largest):
    gain = 1.0
    for axis_at, blocks in pieces:
        steps = jax.random.uniform(jax.random.fold_in(jax.random.fold_in(stream_key, 6), axis_at), (blocks,), jnp.float32, low / len(pieces), largest / len(pieces))
        gain = gain * jnp.repeat(jnp.exp(steps), extent[axis_at] // blocks).reshape((-1,) + (1,) * (len(extent) - 1 - axis_at))
    return gain


def assign_block(stream_key, own, number, rows, number_of, top, bound, slope):
    order = jax.random.permutation(stream_key, number_of)
    heavy_load, usual = shares(number_of, rows * top, bound, slope, True), shares(number_of, rows * top, bound, slope, False)
    places = jnp.arange(number_of)

    def named(sizes, turn):
        used = int((sizes > 0).sum())
        fixed = max(1, used // 4)
        moved = fixed + (places - fixed + turn * (used - fixed)) % max(1, number_of - fixed)
        return jnp.zeros((number_of,), jnp.int32).at[order[jnp.where(places < fixed, places, moved)]].set(jnp.asarray(sizes, jnp.int32))

    sizes = jnp.where(number % 4 == 0, named(heavy_load, number // 4), named(usual, number - number // 4 - 1))
    mixed = jax.random.permutation(jax.random.fold_in(own, 3), number_of)
    source_of, receiver = mixed[0:number_of // 2 * 2:2], mixed[1:number_of // 2 * 2:2]
    margin = jnp.minimum(sizes[source_of] - 1, bound - sizes[receiver]) // 2
    margin = jnp.where((source_of == order[0]) | (receiver == order[0]) | (sizes[receiver] == 0), 0, jnp.maximum(margin, 0))
    moved = jax.random.randint(jax.random.fold_in(own, 4), (number_of // 2,), 0, 1 << 20) % (margin + 1)
    sizes = sizes.at[source_of].add(-moved).at[receiver].add(moved)
    members = jnp.searchsorted(jnp.cumsum(sizes), jnp.arange(rows * top), side="right").astype(jnp.int32)
    grid = members.reshape(top, rows).T
    grid = grid[jax.random.permutation(jax.random.fold_in(own, 1), rows)]
    turn = jax.random.randint(jax.random.fold_in(own, 2), (rows, 1), 0, top)
    return jnp.take_along_axis(grid, (jnp.arange(top)[None, :] + turn) % top, axis=1)


def shares(count, total, most, slope, full):
    weights = [(1 << 20) // math.isqrt(rank ** slope) + 1 for rank in range(1, count + 1)]
    largest = most if full else min(most, max(-(-total // count), total * weights[0] // sum(weights)))
    least = 1 if total - largest >= count - 1 else 0
    counts, surplus = [largest] + [least] * (count - 1), total - largest - least * (count - 1)
    while surplus > 0:
        free = [i for i in range(1, count) if counts[i] < largest] or [i for i in range(1, count) if counts[i] < most]
        mass, left = sum([weights[i] for i in free]), surplus
        for i in free:
            extra = min(most - counts[i], max(1, left * weights[i] // mass), surplus)
            counts[i] = counts[i] + extra
            surplus = surplus - extra
    return np.array(counts)


def normal_values(rng, dims, scale, reach, split=(), held_as=jnp.bfloat16):
    result = jax.random.normal(rng, dims, jnp.float32) * scale
    if len(split) > 0:
        result = levels(rng, dims, split, -0.22, 0.18) * result
    return jnp.clip(result, min=-reach, max=reach).astype(held_as)


def setup_inputs(seed: int = 0) -> dict:
    arg_keys = jax.random.split(jax.random.key(seed), 8)
    tokens = normal_values(arg_keys[0], (TOKENS, D), 1.0, 6.0, ((0, 512),))
    expert_ids_keys = jax.random.split(jax.random.fold_in(arg_keys[1], 1), TOKENS // TOK_DEV)
    expert_ids_turns = jax.random.permutation(jax.random.fold_in(arg_keys[1], 3), TOKENS // TOK_DEV)
    expert_ids = jax.vmap(lambda own, number: assign_block(jax.random.fold_in(arg_keys[1], 2), own, number, TOK_DEV, EXPERTS, TOP, CAP, 2))(expert_ids_keys, expert_ids_turns).reshape((TOKENS, TOP))
    gate_weights = jnp.clip(jnp.exp(math.log(1.0) - 2.3025851 * jax.random.uniform(arg_keys[2], (TOKENS, TOP), jnp.float32) ** levels(arg_keys[2], (TOKENS, TOP), ((0, 512),), -0.2, 0.2)), 0.1, 1.0)
    w_gate = normal_values(arg_keys[3], (N_EP, D, 2 * FF), D ** -0.5, 0.09375, ((0, 32), (2, 16)))
    w_up = normal_values(arg_keys[4], (N_EP, D, 2 * FF), D ** -0.5, 0.09375, ((0, 32), (2, 16)))
    w_down = normal_values(arg_keys[5], (N_EP, FF, 2 * D), FF ** -0.5, 0.1875, ((0, 32), (2, 16)))
    norm_gain = jnp.clip(1.0 + 0.18 * jax.random.normal(arg_keys[6], (D,), jnp.float32), 0.1, 1.9)
    return {"tokens": tokens, "expert_ids": expert_ids, "gate_weights": gate_weights, "w_gate": w_gate, "w_up": w_up, "w_down": w_down, "norm_gain": norm_gain}


def reference(tokens, expert_ids, gate_weights, w_gate, w_up, w_down, norm_gain):
    width = tokens.shape[1]
    hidden_all = w_down.shape[1]
    limit = N_GRP * N_EP * CAP
    experts = 2 * w_gate.shape[0]

    def one_expert(moe, expert):
        hits = expert_ids == expert
        weight = lax.optimization_barrier(jnp.sum(jnp.where(hits, gate_weights, jnp.float32(0.0)), axis=1))
        member = jnp.any(hits, axis=1)
        picked = jnp.nonzero(member, size=limit, fill_value=0)[0].astype(jnp.int32)
        valid = (jnp.arange(limit) < jnp.sum(member.astype(jnp.int32))).astype(jnp.float32)
        rows_in = tokens[picked]
        pair_idx = (expert // 2).astype(jnp.int32)
        half_idx = (expert % 2).astype(jnp.int32)
        gate_pair = lax.dynamic_index_in_dim(w_gate, pair_idx, 0, keepdims=False)
        up_pair = lax.dynamic_index_in_dim(w_up, pair_idx, 0, keepdims=False)
        down_pair = lax.dynamic_index_in_dim(w_down, pair_idx, 0, keepdims=False)
        gate_cols = lax.dynamic_slice_in_dim(gate_pair, half_idx * hidden_all, hidden_all, 1)
        up_cols = lax.dynamic_slice_in_dim(up_pair, half_idx * hidden_all, hidden_all, 1)
        down_cols = lax.dynamic_slice_in_dim(down_pair, half_idx * width, width, 1)
        gate_part = jnp.dot(rows_in, gate_cols, preferred_element_type=jnp.float32)
        up_part = jnp.dot(rows_in, up_cols, preferred_element_type=jnp.float32)
        hidden = (jax.nn.silu(gate_part) * up_part).astype(jnp.bfloat16)
        expert_out = jnp.dot(hidden, down_cols, preferred_element_type=jnp.float32).astype(jnp.bfloat16)
        scale_rows = weight[picked] * valid
        moe = moe.at[picked].add(expert_out.astype(jnp.float32) * scale_rows[:, None])
        return (moe, None)
    start = jnp.zeros(tokens.shape, jnp.float32)
    moe, unused = lax.scan(one_expert, start, jnp.arange(experts, dtype=jnp.int32))
    mixed = tokens.astype(jnp.float32) + moe
    factor = lax.rsqrt(lax.optimization_barrier(jnp.mean(mixed * mixed, axis=1, keepdims=True)) + 1e-06)
    return (mixed * factor * norm_gain).astype(jnp.bfloat16)
```

```python
import jax
import jax.numpy as jnp
from jax import lax
from jax.sharding import PartitionSpec as P

BF16 = jnp.bfloat16
F32 = jnp.float32


def around(block, chips):
    size = lax.axis_size("ep")
    return lax.ppermute(block, "ep", [(i, (i + 2 * chips) % size) for i in range(size)])


def core_swap(block):
    return lax.ppermute(block, "ep", [(i, i ^ 1) for i in range(lax.axis_size("ep"))])


def pair_swap(block):
    return lax.ppermute(block, "grp", [(i, i ^ 4) for i in range(lax.axis_size("grp"))])


EIGHTS = [[0, 1, 2, 3, 12, 13, 14, 15], [4, 5, 6, 7, 8, 9, 10, 11]]
FOURS = [[4 * y + x for x in range(4)] for y in range(4)]


def gather_column(block):
    n = block.shape[0]
    three = jnp.concatenate([block, around(block, 5), around(block, -5)], 0)
    below2, above2 = around(three, 2), around(three, -2)
    eighth = around(three[2 * n:], -3)
    below1, above1 = around(three, 1), around(three, -1)
    column = jnp.concatenate([three, below1, above1, below2, above2, eighth], 0)
    return column


def scatter_group(column, n):
    sent = column[3 * n:].astype(BF16)
    below1, above1, below2, above2 = (sent[3 * n * i:3 * n * (i + 1)] for i in range(4))
    from_above2, from_below2 = around(below2, -2), around(above2, 2)
    eighth = around(sent[12 * n:], 3)
    from_above1, from_below1 = around(below1, -1), around(above1, 1)
    part = column[:3 * n]
    for other in (from_above2, from_below2, from_above1, from_below1):
        part = part + other.astype(F32)
    below = around(part[n:2 * n].astype(BF16), -5)
    above = around((part[2 * n:] + eighth.astype(F32)).astype(BF16), 5)
    return part[:n] + below.astype(F32) + above.astype(F32)


def shards(tokens, expert_ids, gate_weights, w_gate, w_up, w_down, norm_gain):
    n, width = tokens.shape
    top = expert_ids.shape[1]
    g = lax.axis_index("grp")
    p = lax.axis_index("ep")
    odd_row = g // 4 % 2 == 1

    gate_own, up_own, down_own = w_gate[0], w_up[0], w_down[0]
    gate_other, up_other, down_other = pair_swap(gate_own), pair_swap(up_own), pair_swap(down_own)

    high = lax.reduce_precision(gate_weights, 8, 7)
    low = gate_weights - high
    extra = jnp.concatenate([expert_ids.astype(F32), high, low], 1).astype(BF16)
    extra = jnp.pad(extra, ((0, 0), (0, 128 - 3 * top)))
    column = gather_column(jnp.concatenate([tokens, extra], 1))
    column, gate_other = lax.optimization_barrier((column, gate_other))
    parts = column, core_swap(column)
    half = parts[0].shape[0]
    rows = 2 * half
    slots = rows // 4

    take = (jnp.arange(3 * top)[:, None] == jnp.arange(128)[None, :]).astype(BF16)
    facts = [
        lax.dot_general(take, part[:, width:], (((1,), (1,)), ((), ())), preferred_element_type=F32)
        for part in parts
    ]
    facts = jnp.concatenate(facts, 1).reshape(3, top, rows)

    experts = (2 * p + jnp.arange(2)).astype(F32)
    match = facts[0][None] == experts[:, None, None]
    hit = jnp.any(match, axis=1)
    before = jnp.arange(rows)[:, None] < jnp.arange(rows)[None, :]
    place = jnp.dot(hit.astype(BF16), before.astype(BF16), preferred_element_type=F32)
    place = jnp.where(hit, place, -1.0)
    picks = place[:, None, :] == jnp.arange(slots, dtype=F32)[None, :, None]
    picks = picks.reshape(2 * slots, rows)
    onehot = picks.astype(BF16)
    chosen = jnp.dot(onehot[:, :half], parts[0][:, :width], preferred_element_type=F32)
    chosen = chosen + jnp.dot(onehot[:, half:], parts[1][:, :width], preferred_element_type=F32)
    chosen = chosen.astype(BF16)

    fanned = jnp.broadcast_to(chosen.reshape(2, 1, slots, width), (2, 4, slots, width)).reshape(8, slots, width)
    arrived = lax.all_to_all(fanned, "grp", split_axis=0, concat_axis=0, tiled=True, axis_index_groups=EIGHTS)
    arrived = arrived.reshape(8 * slots, width)

    def front(gate, up):
        a = jnp.dot(arrived, gate, preferred_element_type=F32)
        b = jnp.dot(arrived, up, preferred_element_type=F32)
        return (jax.nn.silu(a) * b).astype(BF16)

    mine, theirs = front(gate_own, up_own), front(gate_other, up_other)
    hidden = jnp.where(odd_row, jnp.concatenate([theirs, mine], 1), jnp.concatenate([mine, theirs], 1))
    hidden, down_other = lax.optimization_barrier((hidden, down_other))
    units = mine.shape[1]
    hidden = jnp.broadcast_to(hidden[None], (4,) + hidden.shape)
    hidden = lax.all_to_all(hidden, "grp", split_axis=0, concat_axis=0, tiled=True, axis_index_groups=FOURS)
    hidden = jnp.concatenate(
        [hidden[x, :, units * at:units * (at + 1)] for at in range(2) for x in range(4)], 1
    )

    out_own = jnp.dot(hidden, down_own, preferred_element_type=F32).astype(BF16)
    out_other = jnp.dot(hidden, down_other, preferred_element_type=F32).astype(BF16)
    out = jnp.where(odd_row, jnp.concatenate([out_other, out_own], 1), jnp.concatenate([out_own, out_other], 1))
    features = out_own.shape[1]
    out = out.reshape(8, slots, 2 * features)
    home = lax.all_to_all(out, "grp", split_axis=0, concat_axis=0, tiled=True, axis_index_groups=EIGHTS)
    home = jnp.concatenate(
        [
            jnp.concatenate(
                [home[4 * of + x, :, features * at:features * (at + 1)] for at in range(2) for x in range(4)], 1
            )
            for of in range(2)
        ],
        0,
    )

    def weight(at):
        summed = jnp.sum(jnp.where(match, facts[at][None], 0.0), axis=1)
        summed = jnp.broadcast_to(summed[:, None], (2, slots, rows)).reshape(2 * slots, rows)
        return jnp.where(picks, summed, 0.0).astype(BF16)

    table = jnp.concatenate([weight(1), weight(2)], 0)
    home = jnp.concatenate([home, home], 0)

    def weighted(at):
        return lax.dot_general(at, home, (((0,), (0,)), ((), ())), preferred_element_type=F32)

    swapped = core_swap(weighted(table[:, half:]).astype(BF16))
    column = weighted(table[:, :half]) + swapped.astype(F32)
    mixed = tokens.astype(F32) + scatter_group(column, n)
    factor = lax.rsqrt(jnp.mean(mixed * mixed, axis=1, keepdims=True) + 1e-06)
    return (mixed * factor * norm_gain).astype(BF16)


def solution(mesh):
    placed = (
        P(("grp", "ep"), None),
        P(("grp", "ep"), None),
        P(("grp", "ep"), None),
        P("ep", None, "grp"),
        P("ep", None, "grp"),
        P("ep", None, "grp"),
        P(),
    )
    return jax.shard_map(
        shards, mesh=mesh, in_specs=placed, out_specs=P(("grp", "ep"), None), check_vma=False
    )
```

```python
import jax
import jax.numpy as jnp
from jax import lax
from jax.experimental import pallas as pl
from jax.experimental.pallas import tpu as pltpu
from jax.sharding import PartitionSpec as P

BF16 = jnp.bfloat16
F32 = jnp.float32


def around(block, chips):
    size = lax.axis_size("ep")
    return lax.ppermute(block, "ep", [(i, (i + 2 * chips) % size) for i in range(size)])


def core_swap(block):
    return lax.ppermute(block, "ep", [(i, i ^ 1) for i in range(lax.axis_size("ep"))])


def pair_swap(block):
    return lax.ppermute(block, "grp", [(i, i ^ 4) for i in range(lax.axis_size("grp"))])


EIGHTS = [[0, 1, 2, 3, 12, 13, 14, 15], [4, 5, 6, 7, 8, 9, 10, 11]]
FOURS = [[4 * y + x for x in range(4)] for y in range(4)]


def gather_column(block):
    n = block.shape[0]
    three = jnp.concatenate([block, around(block, 5), around(block, -5)], 0)
    below1, above1 = around(three, 1), around(three, -1)
    eighth = around(three[2 * n:], -3)
    below2, above2 = around(below1, 1), around(above1, -1)
    return jnp.concatenate([three, below1, above1, below2, above2, eighth], 0)


def scatter_group(column, n):
    below1, above1, below2, above2 = (column[3 * n * i:3 * n * (i + 1)] for i in range(1, 5))
    below1 = below1 + around(below2.astype(BF16), -1).astype(F32)
    above1 = above1 + around(above2.astype(BF16), 1).astype(F32)
    eighth = around(column[15 * n:].astype(BF16), 3).astype(F32)
    part = column[:3 * n] + around(below1.astype(BF16), -1).astype(F32) + around(above1.astype(BF16), 1).astype(F32)
    below = around(part[n:2 * n].astype(BF16), -5)
    above = around((part[2 * n:] + eighth).astype(BF16), 5)
    return part[:n] + below.astype(F32) + above.astype(F32)


def whole(shape):
    return pl.BlockSpec(shape, lambda k: (0,) * len(shape))


def pick_rows(onehot, near, other, width):
    picked, half = onehot.shape[0], near.shape[0]
    slots, block = picked // 2, 512

    def kernel(onehot_ref, near_ref, other_ref, out_ref):
        rows = jnp.dot(onehot_ref[:, :half], near_ref[...], preferred_element_type=F32)
        rows = rows + jnp.dot(onehot_ref[:, half:], other_ref[...], preferred_element_type=F32)
        rows = rows.astype(BF16)
        for at in range(8):
            start = at // 4 * slots
            out_ref[at] = rows[start:start + slots]

    return pl.pallas_call(
        kernel,
        grid=(width // block,),
        in_specs=[
            whole(onehot.shape),
            pl.BlockSpec((half, block), lambda k: (0, k)),
            pl.BlockSpec((half, block), lambda k: (0, k)),
        ],
        out_specs=pl.BlockSpec((8, slots, block), lambda k: (0, 0, k)),
        out_shape=jax.ShapeDtypeStruct((8, slots, width), BF16),
        name="pick_rows",
    )(onehot, near, other)


def front(odd, rows, gates, ups):
    count, width = rows.shape
    units, block = gates[0].shape[1], 512
    steps = width // block

    def kernel(odd_ref, rows_ref, gate_own, gate_other, up_own, up_other, out_ref, total):
        k = pl.program_id(0)

        @pl.when(k == 0)
        def _():
            total[...] = jnp.zeros_like(total)

        weights = jnp.concatenate([gate_own[...], gate_other[...], up_own[...], up_other[...]], 1)
        total[...] += jnp.dot(rows_ref[...], weights, preferred_element_type=F32)

        @pl.when(k == steps - 1)
        def _():
            gate, up = total[:, :2 * units], total[:, 2 * units:]
            hidden = gate / (1.0 + jnp.exp(-gate)) * up
            low, high = hidden[:, :units], hidden[:, units:]
            swap = odd_ref[0] == 1
            first, second = jnp.where(swap, high, low).astype(BF16), jnp.where(swap, low, high).astype(BF16)
            for at in range(4):
                out_ref[at, :, :units] = first
                out_ref[at, :, units:] = second

    weight = pl.BlockSpec((block, units), lambda k: (k, 0))
    return pl.pallas_call(
        kernel,
        grid=(steps,),
        in_specs=[
            pl.BlockSpec(memory_space=pltpu.SMEM),
            pl.BlockSpec((count, block), lambda k: (0, k)),
            weight, weight, weight, weight,
        ],
        out_specs=whole((4, count, 2 * units)),
        out_shape=jax.ShapeDtypeStruct((4, count, 2 * units), BF16),
        scratch_shapes=[pltpu.VMEM((count, 4 * units), F32)],
        name="front",
    )(odd, rows, *gates, *ups)


def back(odd, hidden, own, other, slots):
    parts, count, units = hidden.shape
    features = own.shape[1]
    half = units // 2
    own, other = (w.reshape(2, own.shape[0] // 2, features) for w in (own, other))

    def kernel(odd_ref, hidden_ref, own_ref, other_ref, out_ref, total):
        k = pl.program_id(0)

        @pl.when(k == 0)
        def _():
            total[...] = jnp.zeros_like(total)

        weights = [jnp.concatenate([w[0], w[1]], 0) for w in (own_ref, other_ref)]
        total[...] += jnp.dot(hidden_ref[0], jnp.concatenate(weights, 1), preferred_element_type=F32)

        @pl.when(k == parts - 1)
        def _():
            low, high = total[:, :features], total[:, features:]
            swap = odd_ref[0] == 1
            shape = (count // slots, slots, features)
            out_ref[:, :, :features] = jnp.where(swap, high, low).astype(BF16).reshape(shape)
            out_ref[:, :, features:] = jnp.where(swap, low, high).astype(BF16).reshape(shape)

    weight = pl.BlockSpec((2, half, features), lambda k: (0, k, 0))
    out = (count // slots, slots, 2 * features)
    return pl.pallas_call(
        kernel,
        grid=(parts,),
        in_specs=[
            pl.BlockSpec(memory_space=pltpu.SMEM),
            pl.BlockSpec((1, count, units), lambda k: (k, 0, 0)),
            weight, weight,
        ],
        out_specs=whole(out),
        out_shape=jax.ShapeDtypeStruct(out, BF16),
        scratch_shapes=[pltpu.VMEM((count, 2 * features), F32)],
        name="back",
    )(odd, hidden, own, other)


def shards(tokens, expert_ids, gate_weights, w_gate, w_up, w_down, norm_gain):
    n, width = tokens.shape
    top = expert_ids.shape[1]
    g = lax.axis_index("grp")
    p = lax.axis_index("ep")
    odd = (g // 4 % 2).astype(jnp.int32).reshape(1)

    gate_own, up_own, down_own = w_gate[0], w_up[0], w_down[0]
    gate_other, up_other, down_other = pair_swap(gate_own), pair_swap(up_own), pair_swap(down_own)

    high = lax.reduce_precision(gate_weights, 8, 7)
    low = gate_weights - high
    extra = jnp.concatenate([expert_ids.astype(F32), high, low], 1).astype(BF16)
    extra = jnp.pad(extra, ((0, 0), (0, 128 - 3 * top)))
    column = gather_column(jnp.concatenate([tokens, extra], 1))
    column, gate_other, up_other = lax.optimization_barrier((column, gate_other, up_other))
    parts = column, core_swap(column)
    half = parts[0].shape[0]
    rows = 2 * half
    slots = rows // 4

    take = (jnp.arange(3 * top)[:, None] == jnp.arange(128)[None, :]).astype(BF16)
    facts = [
        lax.dot_general(take, part[:, width:], (((1,), (1,)), ((), ())), preferred_element_type=F32)
        for part in parts
    ]
    facts = jnp.concatenate(facts, 1).reshape(3, top, rows)

    experts = (2 * p + jnp.arange(2)).astype(F32)
    match = facts[0][None] == experts[:, None, None]
    hit = jnp.any(match, axis=1)
    before = jnp.arange(rows)[:, None] < jnp.arange(rows)[None, :]
    place = jnp.dot(hit.astype(BF16), before.astype(BF16), preferred_element_type=F32)
    place = jnp.where(hit, place, -1.0)
    picks = place[:, None, :] == jnp.arange(slots, dtype=F32)[None, :, None]
    picks = picks.reshape(2 * slots, rows)
    onehot = picks.astype(BF16)
    fanned = pick_rows(onehot, parts[0], parts[1], width)

    arrived = lax.all_to_all(fanned, "grp", split_axis=0, concat_axis=0, tiled=True, axis_index_groups=EIGHTS)
    arrived = arrived.reshape(8 * slots, width)

    hidden = front(odd, arrived, (gate_own, gate_other), (up_own, up_other))
    hidden, down_other = lax.optimization_barrier((hidden, down_other))
    hidden = lax.all_to_all(hidden, "grp", split_axis=0, concat_axis=0, tiled=True, axis_index_groups=FOURS)

    features = down_own.shape[1]
    out = back(odd, hidden, down_own, down_other, slots)
    home = lax.all_to_all(out, "grp", split_axis=0, concat_axis=0, tiled=True, axis_index_groups=EIGHTS)
    home = jnp.concatenate(
        [
            jnp.concatenate(
                [home[4 * of + x, :, features * at:features * (at + 1)] for at in range(2) for x in range(4)], 1
            )
            for of in range(2)
        ],
        0,
    )

    def weight(at):
        summed = jnp.sum(jnp.where(match, facts[at][None], 0.0), axis=1)
        summed = jnp.broadcast_to(summed[:, None], (2, slots, rows)).reshape(2 * slots, rows)
        return jnp.where(picks, summed, 0.0).astype(BF16)

    table = jnp.concatenate([weight(1), weight(2)], 0)
    home = jnp.concatenate([home, home], 0)

    def weighted(at):
        return lax.dot_general(at, home, (((0,), (0,)), ((), ())), preferred_element_type=F32)

    swapped = core_swap(weighted(table[:, half:]).astype(BF16))
    column = weighted(table[:, :half]) + swapped.astype(F32)
    mixed = tokens.astype(F32) + scatter_group(column, n)
    factor = lax.rsqrt(jnp.mean(mixed * mixed, axis=1, keepdims=True) + 1e-06)
    return (mixed * factor * norm_gain).astype(BF16)


def solution(mesh):
    placed = (
        P(("grp", "ep"), None),
        P(("grp", "ep"), None),
        P(("grp", "ep"), None),
        P("ep", None, "grp"),
        P("ep", None, "grp"),
        P("ep", None, "grp"),
        P(),
    )
    return jax.shard_map(
        shards, mesh=mesh, in_specs=placed, out_specs=P(("grp", "ep"), None), check_vma=False
    )
```

```python
import jax
import jax.numpy as jnp
from jax import lax
from jax.experimental import pallas as pl
from jax.experimental.pallas import tpu as pltpu
from jax.sharding import PartitionSpec as P

BF16 = jnp.bfloat16
F32 = jnp.float32


def around(block, chips):
    size = lax.axis_size("ep")
    return lax.ppermute(block, "ep", [(i, (i + 2 * chips) % size) for i in range(size)])


def core_swap(block):
    return lax.ppermute(block, "ep", [(i, i ^ 1) for i in range(lax.axis_size("ep"))])


def pair_swap(block):
    return lax.ppermute(block, "grp", [(i, i ^ 4) for i in range(lax.axis_size("grp"))])


EIGHTS = [[0, 1, 2, 3, 12, 13, 14, 15], [4, 5, 6, 7, 8, 9, 10, 11]]
FOURS = [[4 * y + x for x in range(4)] for y in range(4)]


def gather_column(block):
    n = block.shape[0]
    three = jnp.concatenate([block, around(block, 5), around(block, -5)], 0)
    below1, above1 = around(three, 1), around(three, -1)
    eighth = around(three[2 * n:], -3)
    below2, above2 = around(below1, 1), around(above1, -1)
    return jnp.concatenate([three, below1, above1, below2, above2, eighth], 0)


def scatter_group(column, n):
    sent = column[3 * n:].astype(BF16)
    below1, above1, below2, above2 = (sent[3 * n * i:3 * n * (i + 1)] for i in range(4))
    from_above2, from_below2 = around(below2, -2), around(above2, 2)
    eighth = around(sent[12 * n:], 3)
    from_above1, from_below1 = around(below1, -1), around(above1, 1)
    part = column[:3 * n]
    for other in (from_above2, from_below2, from_above1, from_below1):
        part = part + other.astype(F32)
    below = around(part[n:2 * n].astype(BF16), -5)
    above = around((part[2 * n:] + eighth.astype(F32)).astype(BF16), 5)
    return part[:n] + below.astype(F32) + above.astype(F32)


def whole(shape):
    return pl.BlockSpec(shape, lambda k: (0,) * len(shape))


def front(odd, rows, gates, ups):
    count, width = rows.shape
    units, block = gates[0].shape[1], 1024
    steps = width // block

    def kernel(odd_ref, rows_ref, gate_own, gate_other, up_own, up_first, up_last, out_ref, total):
        k = pl.program_id(0)

        @pl.when(k == 0)
        def _():
            total[...] = jnp.zeros_like(total)

        up_other = jnp.where(k < steps // 2, up_first[...], up_last[...])
        weights = jnp.concatenate([gate_own[...], gate_other[...], up_own[...], up_other], 1)
        total[...] += jnp.dot(rows_ref[...], weights, preferred_element_type=F32)

        @pl.when(k == steps - 1)
        def _():
            gate, up = total[:, :2 * units], total[:, 2 * units:]
            hidden = gate / (1.0 + jnp.exp(-gate)) * up
            low, high = hidden[:, :units], hidden[:, units:]
            swap = odd_ref[0] == 1
            first, second = jnp.where(swap, high, low).astype(BF16), jnp.where(swap, low, high).astype(BF16)
            for at in range(4):
                out_ref[at, :, :units] = first
                out_ref[at, :, units:] = second

    weight = pl.BlockSpec((block, units), lambda k: (k, 0))
    return pl.pallas_call(
        kernel,
        grid=(steps,),
        in_specs=[
            pl.BlockSpec(memory_space=pltpu.SMEM),
            pl.BlockSpec((count, block), lambda k: (0, k)),
            weight, weight, weight,
            pl.BlockSpec((block, units), lambda k: (jnp.minimum(k, steps // 2 - 1), 0)),
            pl.BlockSpec((block, units), lambda k: (jnp.maximum(k - steps // 2, 0), 0)),
        ],
        out_specs=whole((4, count, 2 * units)),
        out_shape=jax.ShapeDtypeStruct((4, count, 2 * units), BF16),
        scratch_shapes=[pltpu.VMEM((count, 4 * units), F32)],
        name="front",
    )(odd, rows, *gates, *ups)


def back(odd, hidden, own, other, slots):
    parts, count, units = hidden.shape
    features = own.shape[1]
    half, steps = units // 2, parts // 2
    own, other = (w.reshape(2, own.shape[0] // 2, features) for w in (own, other))

    def kernel(odd_ref, hidden_ref, own_ref, other_ref, out_ref, total):
        k = pl.program_id(0)

        @pl.when(k == 0)
        def _():
            total[...] = jnp.zeros_like(total)

        weights = [
            jnp.concatenate([w[at, j * half:(j + 1) * half] for j in range(2) for at in range(2)], 0)
            for w in (own_ref, other_ref)
        ]
        rows = jnp.concatenate([hidden_ref[0], hidden_ref[1]], 1)
        total[...] += jnp.dot(rows, jnp.concatenate(weights, 1), preferred_element_type=F32)

        @pl.when(k == steps - 1)
        def _():
            low, high = total[:, :features], total[:, features:]
            swap = odd_ref[0] == 1
            shape = (count // slots, slots, features)
            out_ref[:, :, :features] = jnp.where(swap, high, low).astype(BF16).reshape(shape)
            out_ref[:, :, features:] = jnp.where(swap, low, high).astype(BF16).reshape(shape)

    weight = pl.BlockSpec((2, 2 * half, features), lambda k: (0, k, 0))
    out = (count // slots, slots, 2 * features)
    return pl.pallas_call(
        kernel,
        grid=(steps,),
        in_specs=[
            pl.BlockSpec(memory_space=pltpu.SMEM),
            pl.BlockSpec((2, count, units), lambda k: (k, 0, 0)),
            weight, weight,
        ],
        out_specs=whole(out),
        out_shape=jax.ShapeDtypeStruct(out, BF16),
        scratch_shapes=[pltpu.VMEM((count, 2 * features), F32)],
        name="back",
    )(odd, hidden, own, other)


def shards(tokens, expert_ids, gate_weights, w_gate, w_up, w_down, norm_gain):
    n, width = tokens.shape
    top = expert_ids.shape[1]
    g = lax.axis_index("grp")
    p = lax.axis_index("ep")
    odd = (g // 4 % 2).astype(jnp.int32).reshape(1)

    gate_own, up_own, down_own = w_gate[0], w_up[0], w_down[0]
    middle = width // 2
    gate_other, up_first, up_last = pair_swap(gate_own), pair_swap(up_own[:middle]), pair_swap(up_own[middle:])

    high = lax.reduce_precision(gate_weights, 8, 7)
    low = gate_weights - high
    extra = jnp.concatenate([expert_ids.astype(F32), high, low], 1).astype(BF16)
    extra = jnp.pad(extra, ((0, 0), (0, 128 - 3 * top)))
    column = gather_column(jnp.concatenate([tokens, extra], 1))
    column, gate_other, up_first = lax.optimization_barrier((column, gate_other, up_first))
    parts = column, core_swap(column)
    half = parts[0].shape[0]
    rows = 2 * half
    slots = rows // 4

    take = (jnp.arange(3 * top)[:, None] == jnp.arange(128)[None, :]).astype(BF16)
    facts = [
        lax.dot_general(take, part[:, width:], (((1,), (1,)), ((), ())), preferred_element_type=F32)
        for part in parts
    ]
    facts = jnp.concatenate(facts, 1).reshape(3, top, rows)

    experts = (2 * p + jnp.arange(2)).astype(F32)
    match = facts[0][None] == experts[:, None, None]
    hit = jnp.any(match, axis=1)
    before = jnp.arange(rows)[:, None] < jnp.arange(rows)[None, :]
    place = jnp.dot(hit.astype(BF16), before.astype(BF16), preferred_element_type=F32)
    place = jnp.where(hit, place, -1.0)
    picks = place[:, None, :] == jnp.arange(slots, dtype=F32)[None, :, None]
    picks = picks.reshape(2 * slots, rows)
    onehot = picks.astype(BF16)
    chosen = jnp.dot(onehot[:, :half], parts[0][:, :width], preferred_element_type=F32)
    chosen = chosen + jnp.dot(onehot[:, half:], parts[1][:, :width], preferred_element_type=F32)
    chosen = chosen.astype(BF16).reshape(2, 1, slots, width)
    fanned = jnp.broadcast_to(chosen, (2, 4, slots, width)).reshape(8, slots, width)
    fanned, up_last = lax.optimization_barrier((fanned, up_last))

    arrived = lax.all_to_all(fanned, "grp", split_axis=0, concat_axis=0, tiled=True, axis_index_groups=EIGHTS)
    arrived, down_own = lax.optimization_barrier((arrived, down_own))
    down_other = pair_swap(down_own)
    arrived = arrived.reshape(8 * slots, width)

    hidden = front(odd, arrived, (gate_own, gate_other), (up_own, up_first, up_last))
    hidden = lax.all_to_all(hidden, "grp", split_axis=0, concat_axis=0, tiled=True, axis_index_groups=FOURS)

    features = down_own.shape[1]
    out = back(odd, hidden, down_own, down_other, slots)
    home = lax.all_to_all(out, "grp", split_axis=0, concat_axis=0, tiled=True, axis_index_groups=EIGHTS)
    home = jnp.concatenate(
        [
            jnp.concatenate(
                [home[4 * of + x, :, features * at:features * (at + 1)] for at in range(2) for x in range(4)], 1
            )
            for of in range(2)
        ],
        0,
    )

    def weight(at):
        summed = jnp.sum(jnp.where(match, facts[at][None], 0.0), axis=1)
        summed = jnp.broadcast_to(summed[:, None], (2, slots, rows)).reshape(2 * slots, rows)
        return jnp.where(picks, summed, 0.0).astype(BF16)

    table = jnp.concatenate([weight(1), weight(2)], 0)
    home = jnp.concatenate([home, home], 0)

    def weighted(at):
        return lax.dot_general(at, home, (((0,), (0,)), ((), ())), preferred_element_type=F32)

    swapped = core_swap(weighted(table[:, half:]).astype(BF16))
    column = weighted(table[:, :half]) + swapped.astype(F32)
    mixed = tokens.astype(F32) + scatter_group(column, n)
    factor = lax.rsqrt(jnp.mean(mixed * mixed, axis=1, keepdims=True) + 1e-06)
    return (mixed * factor * norm_gain).astype(BF16)


def solution(mesh):
    placed = (
        P(("grp", "ep"), None),
        P(("grp", "ep"), None),
        P(("grp", "ep"), None),
        P("ep", None, "grp"),
        P("ep", None, "grp"),
        P("ep", None, "grp"),
        P(),
    )
    return jax.shard_map(
        shards, mesh=mesh, in_specs=placed, out_specs=P(("grp", "ep"), None), check_vma=False
    )
```

```python
import jax
import jax.numpy as jnp
from jax import lax
from jax.experimental import pallas as pl
from jax.experimental.pallas import tpu as pltpu
from jax.sharding import PartitionSpec as P

BF16 = jnp.bfloat16
F32 = jnp.float32


def around(block, chips):
    size = lax.axis_size("ep")
    return lax.ppermute(block, "ep", [(i, (i + 2 * chips) % size) for i in range(size)])


def core_swap(block):
    return lax.ppermute(block, "ep", [(i, i ^ 1) for i in range(lax.axis_size("ep"))])


def pair_swap(block):
    return lax.ppermute(block, "grp", [(i, i ^ 4) for i in range(lax.axis_size("grp"))])


EIGHTS = [[0, 1, 2, 3, 12, 13, 14, 15], [4, 5, 6, 7, 8, 9, 10, 11]]
FOURS = [[4 * y + x for x in range(4)] for y in range(4)]


def gather_column(block):
    n = block.shape[0]
    three = jnp.concatenate([block, around(block, 5), around(block, -5)], 0)
    below1, above1 = around(three, 1), around(three, -1)
    eighth = around(three[2 * n:], -3)
    below2, above2 = around(below1, 1), around(above1, -1)
    return jnp.concatenate([three, below1, above1, below2, above2, eighth], 0)


def scatter_group(column, n):
    sent = column[3 * n:].astype(BF16)
    below1, above1, below2, above2 = (sent[3 * n * i:3 * n * (i + 1)] for i in range(4))
    from_above2, from_below2 = around(below2, -2), around(above2, 2)
    eighth = around(sent[12 * n:], 3)
    from_above1, from_below1 = around(below1, -1), around(above1, 1)
    part = column[:3 * n]
    for other in (from_above2, from_below2, from_above1, from_below1):
        part = part + other.astype(F32)
    below = around(part[n:2 * n].astype(BF16), -5)
    above = around((part[2 * n:] + eighth.astype(F32)).astype(BF16), 5)
    return part[:n] + below.astype(F32) + above.astype(F32)


def whole(shape):
    return pl.BlockSpec(shape, lambda k: (0,) * len(shape))


def with_facts(tokens, ids, weights):
    n, width = tokens.shape
    top = ids.shape[1]

    def kernel(tokens_ref, ids_ref, weights_ref, out_ref):
        out_ref[:, :width] = tokens_ref[...]
        named = ids_ref[...].astype(F32).astype(BF16)
        high = weights_ref[...].astype(BF16)
        low = (weights_ref[...] - high.astype(F32)).astype(BF16)
        lane = lax.broadcasted_iota(jnp.int32, (top, 128), 1)
        row = lax.broadcasted_iota(jnp.int32, (top, 128), 0)
        facts = jnp.zeros((n, 128), F32)
        for at, part in enumerate((named, high, low)):
            place = jnp.where(lane == row + at * top, 1.0, 0.0).astype(BF16)
            facts = facts + jnp.dot(part, place, preferred_element_type=F32)
        out_ref[:, width:] = facts.astype(BF16)

    return pl.pallas_call(
        kernel, out_shape=jax.ShapeDtypeStruct((n, width + 128), BF16), name="with_facts"
    )(tokens, ids, weights)


def front(odd, rows, gates, ups):
    count, width = rows.shape
    units, block = gates[0].shape[1], 1024
    steps = width // block

    def kernel(odd_ref, rows_ref, gate_own, gate_other, up_own, up_other, out_ref, total):
        k = pl.program_id(0)

        @pl.when(k == 0)
        def _():
            total[...] = jnp.zeros_like(total)

        weights = jnp.concatenate([gate_own[...], gate_other[...], up_own[...], up_other[...]], 1)
        total[...] += jnp.dot(rows_ref[...], weights, preferred_element_type=F32)

        @pl.when(k == steps - 1)
        def _():
            gate, up = total[:, :2 * units], total[:, 2 * units:]
            hidden = gate / (1.0 + jnp.exp(-gate)) * up
            low, high = hidden[:, :units], hidden[:, units:]
            swap = odd_ref[0] == 1
            first, second = jnp.where(swap, high, low).astype(BF16), jnp.where(swap, low, high).astype(BF16)
            for at in range(4):
                out_ref[at, :, :units] = first
                out_ref[at, :, units:] = second

    weight = pl.BlockSpec((block, units), lambda k: (k, 0))
    return pl.pallas_call(
        kernel,
        grid=(steps,),
        in_specs=[
            pl.BlockSpec(memory_space=pltpu.SMEM),
            pl.BlockSpec((count, block), lambda k: (0, k)),
            weight, weight, weight, weight,
        ],
        out_specs=whole((4, count, 2 * units)),
        out_shape=jax.ShapeDtypeStruct((4, count, 2 * units), BF16),
        scratch_shapes=[pltpu.VMEM((count, 4 * units), F32)],
        name="front",
    )(odd, rows, *gates, *ups)


def back(odd, hidden, own, other, slots):
    parts, count, units = hidden.shape
    features = own.shape[1]
    half, steps = units // 2, parts // 2
    own, other = (w.reshape(2, own.shape[0] // 2, features) for w in (own, other))

    def kernel(odd_ref, hidden_ref, own_ref, other_ref, out_ref, total):
        k = pl.program_id(0)

        @pl.when(k == 0)
        def _():
            total[...] = jnp.zeros_like(total)

        weights = [
            jnp.concatenate([w[at, j * half:(j + 1) * half] for j in range(2) for at in range(2)], 0)
            for w in (own_ref, other_ref)
        ]
        rows = jnp.concatenate([hidden_ref[0], hidden_ref[1]], 1)
        total[...] += jnp.dot(rows, jnp.concatenate(weights, 1), preferred_element_type=F32)

        @pl.when(k == steps - 1)
        def _():
            low, high = total[:, :features], total[:, features:]
            swap = odd_ref[0] == 1
            shape = (count // slots, slots, features)
            out_ref[:, :, :features] = jnp.where(swap, high, low).astype(BF16).reshape(shape)
            out_ref[:, :, features:] = jnp.where(swap, low, high).astype(BF16).reshape(shape)

    weight = pl.BlockSpec((2, 2 * half, features), lambda k: (0, k, 0))
    out = (count // slots, slots, 2 * features)
    return pl.pallas_call(
        kernel,
        grid=(steps,),
        in_specs=[
            pl.BlockSpec(memory_space=pltpu.SMEM),
            pl.BlockSpec((2, count, units), lambda k: (k, 0, 0)),
            weight, weight,
        ],
        out_specs=whole(out),
        out_shape=jax.ShapeDtypeStruct(out, BF16),
        scratch_shapes=[pltpu.VMEM((count, 2 * features), F32)],
        name="back",
    )(odd, hidden, own, other)


def shards(tokens, expert_ids, gate_weights, w_gate, w_up, w_down, norm_gain):
    n, width = tokens.shape
    top = expert_ids.shape[1]
    g = lax.axis_index("grp")
    p = lax.axis_index("ep")
    odd = (g // 4 % 2).astype(jnp.int32).reshape(1)

    gate_own, up_own, down_own = w_gate[0], w_up[0], w_down[0]
    gate_other, up_other, down_other = pair_swap(gate_own), pair_swap(up_own), pair_swap(down_own)

    column = gather_column(with_facts(tokens, expert_ids, gate_weights))
    parts = column, core_swap(column)
    half = parts[0].shape[0]
    rows = 2 * half
    slots = rows // 4

    take = (jnp.arange(3 * top)[:, None] == jnp.arange(128)[None, :]).astype(BF16)
    facts = [
        lax.dot_general(take, part[:, width:], (((1,), (1,)), ((), ())), preferred_element_type=F32)
        for part in parts
    ]
    facts = jnp.concatenate(facts, 1).reshape(3, top, rows)

    experts = (2 * p + jnp.arange(2)).astype(F32)
    match = facts[0][None] == experts[:, None, None]
    hit = jnp.any(match, axis=1)
    before = jnp.arange(rows)[:, None] < jnp.arange(rows)[None, :]
    place = jnp.dot(hit.astype(BF16), before.astype(BF16), preferred_element_type=F32)
    place = jnp.where(hit, place, -1.0)
    picks = place[:, None, :] == jnp.arange(slots, dtype=F32)[None, :, None]
    picks = picks.reshape(2 * slots, rows)
    onehot = picks.astype(BF16)
    chosen = jnp.dot(onehot[:, :half], parts[0][:, :width], preferred_element_type=F32)
    chosen = chosen + jnp.dot(onehot[:, half:], parts[1][:, :width], preferred_element_type=F32)
    chosen = chosen.astype(BF16).reshape(2, 1, slots, width)
    fanned = jnp.broadcast_to(chosen, (2, 4, slots, width)).reshape(8, slots, width)

    arrived = lax.all_to_all(fanned, "grp", split_axis=0, concat_axis=0, tiled=True, axis_index_groups=EIGHTS)
    arrived = arrived.reshape(8 * slots, width)

    hidden = front(odd, arrived, (gate_own, gate_other), (up_own, up_other))
    hidden, down_other = lax.optimization_barrier((hidden, down_other))
    hidden = lax.all_to_all(hidden, "grp", split_axis=0, concat_axis=0, tiled=True, axis_index_groups=FOURS)

    features = down_own.shape[1]
    out = back(odd, hidden, down_own, down_other, slots)
    home = lax.all_to_all(out, "grp", split_axis=0, concat_axis=0, tiled=True, axis_index_groups=EIGHTS)
    home = jnp.concatenate(
        [
            jnp.concatenate(
                [home[4 * of + x, :, features * at:features * (at + 1)] for at in range(2) for x in range(4)], 1
            )
            for of in range(2)
        ],
        0,
    )

    def weight(at):
        summed = jnp.sum(jnp.where(match, facts[at][None], 0.0), axis=1)
        summed = jnp.broadcast_to(summed[:, None], (2, slots, rows)).reshape(2 * slots, rows)
        return jnp.where(picks, summed, 0.0).astype(BF16)

    table = jnp.concatenate([weight(1), weight(2)], 0)
    home = jnp.concatenate([home, home], 0)

    def weighted(at):
        return lax.dot_general(at, home, (((0,), (0,)), ((), ())), preferred_element_type=F32)

    swapped = core_swap(weighted(table[:, half:]).astype(BF16))
    column = weighted(table[:, :half]) + swapped.astype(F32)
    mixed = tokens.astype(F32) + scatter_group(column, n)
    factor = lax.rsqrt(jnp.mean(mixed * mixed, axis=1, keepdims=True) + 1e-06)
    return (mixed * factor * norm_gain).astype(BF16)


def solution(mesh):
    placed = (
        P(("grp", "ep"), None),
        P(("grp", "ep"), None),
        P(("grp", "ep"), None),
        P("ep", None, "grp"),
        P("ep", None, "grp"),
        P("ep", None, "grp"),
        P(),
    )
    return jax.shard_map(
        shards, mesh=mesh, in_specs=placed, out_specs=P(("grp", "ep"), None), check_vma=False
    )
```

```python
import jax
import jax.numpy as jnp
from jax import lax
from jax.experimental import pallas as pl
from jax.experimental.pallas import tpu as pltpu
from jax.sharding import PartitionSpec as P

BF16 = jnp.bfloat16
F32 = jnp.float32


def around(block, chips):
    size = lax.axis_size("ep")
    return lax.ppermute(block, "ep", [(i, (i + 2 * chips) % size) for i in range(size)])


def core_swap(block):
    return lax.ppermute(block, "ep", [(i, i ^ 1) for i in range(lax.axis_size("ep"))])


def pair_swap(block):
    return lax.ppermute(block, "grp", [(i, i ^ 1) for i in range(lax.axis_size("grp"))])


EIGHTS = [[4 * y + x for y in range(4) for x in pair] for pair in ((0, 3), (1, 2))]
FOURS = [group[at:at + 4] for group in EIGHTS for at in (0, 4)]


def gather_column(block):
    n = block.shape[0]
    three = jnp.concatenate([block, around(block, 5), around(block, -5)], 0)
    below1, above1 = around(three, 1), around(three, -1)
    eighth = around(three[2 * n:], -3)
    below2, above2 = around(below1, 1), around(above1, -1)
    return jnp.concatenate([three, below1, above1, below2, above2, eighth], 0)


def scatter_group(column, n):
    sent = column[3 * n:].astype(BF16)
    below1, above1, below2, above2 = (sent[3 * n * i:3 * n * (i + 1)] for i in range(4))
    from_above2, from_below2 = around(below2, -2), around(above2, 2)
    eighth = around(sent[12 * n:], 3)
    from_above1, from_below1 = around(below1, -1), around(above1, 1)
    part = column[:3 * n]
    for other in (from_above2, from_below2, from_above1, from_below1):
        part = part + other.astype(F32)
    below = around(part[n:2 * n].astype(BF16), -5)
    above = around((part[2 * n:] + eighth.astype(F32)).astype(BF16), 5)
    return part[:n] + below.astype(F32) + above.astype(F32)


def whole(shape):
    return pl.BlockSpec(shape, lambda k: (0,) * len(shape))


def with_facts(tokens, ids, weights):
    n, width = tokens.shape
    top = ids.shape[1]

    def kernel(tokens_ref, ids_ref, weights_ref, out_ref):
        out_ref[:, :width] = tokens_ref[...]
        named = ids_ref[...].astype(F32).astype(BF16)
        high = weights_ref[...].astype(BF16)
        low = (weights_ref[...] - high.astype(F32)).astype(BF16)
        lane = lax.broadcasted_iota(jnp.int32, (top, 128), 1)
        row = lax.broadcasted_iota(jnp.int32, (top, 128), 0)
        facts = jnp.zeros((n, 128), F32)
        for at, part in enumerate((named, high, low)):
            place = jnp.where(lane == row + at * top, 1.0, 0.0).astype(BF16)
            facts = facts + jnp.dot(part, place, preferred_element_type=F32)
        out_ref[:, width:] = facts.astype(BF16)

    return pl.pallas_call(
        kernel, out_shape=jax.ShapeDtypeStruct((n, width + 128), BF16), name="with_facts"
    )(tokens, ids, weights)


def front(odd, rows, gates, ups):
    count, width = rows.shape
    units, block = gates[0].shape[1], 1024
    steps = width // block

    def kernel(odd_ref, rows_ref, gate_own, gate_other, up_own, up_other, out_ref, total):
        k = pl.program_id(0)

        @pl.when(k == 0)
        def _():
            total[...] = jnp.zeros_like(total)

        weights = jnp.concatenate([gate_own[...], gate_other[...], up_own[...], up_other[...]], 1)
        total[...] += jnp.dot(rows_ref[...], weights, preferred_element_type=F32)

        @pl.when(k == steps - 1)
        def _():
            gate, up = total[:, :2 * units], total[:, 2 * units:]
            hidden = gate / (1.0 + jnp.exp(-gate)) * up
            low, high = hidden[:, :units], hidden[:, units:]
            swap = odd_ref[0] == 1
            first, second = jnp.where(swap, high, low).astype(BF16), jnp.where(swap, low, high).astype(BF16)
            for at in range(4):
                out_ref[at, :, :units] = first
                out_ref[at, :, units:] = second

    weight = pl.BlockSpec((block, units), lambda k: (k, 0))
    return pl.pallas_call(
        kernel,
        grid=(steps,),
        in_specs=[
            pl.BlockSpec(memory_space=pltpu.SMEM),
            pl.BlockSpec((count, block), lambda k: (0, k)),
            weight, weight, weight, weight,
        ],
        out_specs=whole((4, count, 2 * units)),
        out_shape=jax.ShapeDtypeStruct((4, count, 2 * units), BF16),
        scratch_shapes=[pltpu.VMEM((count, 4 * units), F32)],
        name="front",
    )(odd, rows, *gates, *ups)


def back(odd, hidden, own, other, slots):
    parts, count, units = hidden.shape
    features = own.shape[1]
    steps = parts // 2

    def kernel(odd_ref, hidden_ref, own_ref, other_ref, out_ref, total):
        k = pl.program_id(0)

        @pl.when(k == 0)
        def _():
            total[...] = jnp.zeros_like(total)

        rows = jnp.concatenate([hidden_ref[0], hidden_ref[1]], 1)
        weights = jnp.concatenate([own_ref[...], other_ref[...]], 1)
        total[...] += jnp.dot(rows, weights, preferred_element_type=F32)

        @pl.when(k == steps - 1)
        def _():
            low, high = total[:, :features], total[:, features:]
            swap = odd_ref[0] == 1
            shape = (count // slots, slots, features)
            out_ref[:, :, :features] = jnp.where(swap, high, low).astype(BF16).reshape(shape)
            out_ref[:, :, features:] = jnp.where(swap, low, high).astype(BF16).reshape(shape)

    weight = pl.BlockSpec((2 * units, features), lambda k: (k, 0))
    out = (count // slots, slots, 2 * features)
    return pl.pallas_call(
        kernel,
        grid=(steps,),
        in_specs=[
            pl.BlockSpec(memory_space=pltpu.SMEM),
            pl.BlockSpec((2, count, units), lambda k: (k, 0, 0)),
            weight, weight,
        ],
        out_specs=whole(out),
        out_shape=jax.ShapeDtypeStruct(out, BF16),
        scratch_shapes=[pltpu.VMEM((count, 2 * features), F32)],
        name="back",
    )(odd, hidden, own, other)


def shards(tokens, expert_ids, gate_weights, w_gate, w_up, w_down, norm_gain):
    n, width = tokens.shape
    top = expert_ids.shape[1]
    g = lax.axis_index("grp")
    p = lax.axis_index("ep")
    odd = (g % 2).astype(jnp.int32).reshape(1)

    gate_own, up_own, down_own = w_gate[0], w_up[0], w_down[0]
    gate_other, up_other, down_other = pair_swap(gate_own), pair_swap(up_own), pair_swap(down_own)

    column = gather_column(with_facts(tokens, expert_ids, gate_weights))
    column, gate_other = lax.optimization_barrier((column, gate_other))
    parts = column, core_swap(column)
    half = parts[0].shape[0]
    rows = 2 * half
    slots = rows // 4

    take = (jnp.arange(3 * top)[:, None] == jnp.arange(128)[None, :]).astype(BF16)
    facts = [
        lax.dot_general(take, part[:, width:], (((1,), (1,)), ((), ())), preferred_element_type=F32)
        for part in parts
    ]
    facts = jnp.concatenate(facts, 1).reshape(3, top, rows)

    experts = (2 * p + jnp.arange(2)).astype(F32)
    match = facts[0][None] == experts[:, None, None]
    hit = jnp.any(match, axis=1)
    before = jnp.arange(rows)[:, None] < jnp.arange(rows)[None, :]
    place = jnp.dot(hit.astype(BF16), before.astype(BF16), preferred_element_type=F32)
    place = jnp.where(hit, place, -1.0)
    picks = place[:, None, :] == jnp.arange(slots, dtype=F32)[None, :, None]
    picks = picks.reshape(2 * slots, rows)
    onehot = picks.astype(BF16)
    chosen = jnp.dot(onehot[:, :half], parts[0][:, :width], preferred_element_type=F32)
    chosen = chosen + jnp.dot(onehot[:, half:], parts[1][:, :width], preferred_element_type=F32)
    chosen = chosen.astype(BF16).reshape(2, 1, slots, width)
    fanned = jnp.broadcast_to(chosen, (2, 4, slots, width)).reshape(8, slots, width)

    arrived = lax.all_to_all(fanned, "grp", split_axis=0, concat_axis=0, tiled=True, axis_index_groups=EIGHTS)
    arrived = arrived.reshape(8 * slots, width)

    hidden = front(odd, arrived, (gate_own, gate_other), (up_own, up_other))
    hidden, down_other = lax.optimization_barrier((hidden, down_other))
    hidden = lax.all_to_all(hidden, "grp", split_axis=0, concat_axis=0, tiled=True, axis_index_groups=FOURS)

    out = back(odd, hidden, down_own, down_other, slots)
    home = lax.all_to_all(out, "grp", split_axis=0, concat_axis=0, tiled=True, axis_index_groups=EIGHTS)
    home = jnp.concatenate([jnp.concatenate(list(home[at:at + 4]), 1) for at in (0, 4)], 0)

    def weight(at):
        summed = jnp.sum(jnp.where(match, facts[at][None], 0.0), axis=1)
        summed = jnp.broadcast_to(summed[:, None], (2, slots, rows)).reshape(2 * slots, rows)
        return jnp.where(picks, summed, 0.0).astype(BF16)

    table = jnp.concatenate([weight(1), weight(2)], 0)
    home = jnp.concatenate([home, home], 0)

    def weighted(at):
        return lax.dot_general(at, home, (((0,), (0,)), ((), ())), preferred_element_type=F32)

    swapped = core_swap(weighted(table[:, half:]).astype(BF16))
    column = weighted(table[:, :half]) + swapped.astype(F32)
    mixed = tokens.astype(F32) + scatter_group(column, n)
    factor = lax.rsqrt(jnp.mean(mixed * mixed, axis=1, keepdims=True) + 1e-06)
    return (mixed * factor * norm_gain).astype(BF16)


def solution(mesh):
    placed = (
        P(("grp", "ep"), None),
        P(("grp", "ep"), None),
        P(("grp", "ep"), None),
        P("ep", None, "grp"),
        P("ep", None, "grp"),
        P("ep", None, "grp"),
        P(),
    )
    return jax.shard_map(
        shards, mesh=mesh, in_specs=placed, out_specs=P(("grp", "ep"), None), check_vma=False
    )
```

```python
import jax
import jax.numpy as jnp
from jax import lax
from jax.experimental import pallas as pl
from jax.experimental.pallas import tpu as pltpu
from jax.sharding import PartitionSpec as P

BF16 = jnp.bfloat16
F32 = jnp.float32


def around(block, chips):
    size = lax.axis_size("ep")
    return lax.ppermute(block, "ep", [(i, (i + 2 * chips) % size) for i in range(size)])


def core_swap(block):
    return lax.ppermute(block, "ep", [(i, i ^ 1) for i in range(lax.axis_size("ep"))])


def pair_swap(block):
    return lax.ppermute(block, "grp", [(i, i ^ 1) for i in range(lax.axis_size("grp"))])


EIGHTS = [[4 * y + x for y in range(4) for x in pair] for pair in ((0, 3), (1, 2))]
FOURS = [group[at:at + 4] for group in EIGHTS for at in (0, 4)]


def gather_column(block):
    n = block.shape[0]
    three = jnp.concatenate([block, around(block, 5), around(block, -5)], 0)
    below1, above1 = around(three, 1), around(three, -1)
    eighth = around(three[2 * n:], -3)
    below2, above2 = around(below1, 1), around(above1, -1)
    return jnp.concatenate([three, below1, above1, below2, above2, eighth], 0)


def scatter_group(column, n):
    sent = column[3 * n:].astype(BF16)
    below1, above1, below2, above2 = (sent[3 * n * i:3 * n * (i + 1)] for i in range(4))
    from_above2, from_below2 = around(below2, -2), around(above2, 2)
    eighth = around(sent[12 * n:], 3)
    from_above1, from_below1 = around(below1, -1), around(above1, 1)
    part = column[:3 * n]
    for other in (from_above2, from_below2, from_above1, from_below1):
        part = part + other.astype(F32)
    below = around(part[n:2 * n].astype(BF16), -5)
    above = around((part[2 * n:] + eighth.astype(F32)).astype(BF16), 5)
    return part[:n] + below.astype(F32) + above.astype(F32)


def whole(shape):
    return pl.BlockSpec(shape, lambda k: (0,) * len(shape))


def with_facts(tokens, ids, weights):
    n, width = tokens.shape
    top = ids.shape[1]

    def kernel(tokens_ref, ids_ref, weights_ref, out_ref):
        out_ref[:, :width] = tokens_ref[...]
        named = ids_ref[...].astype(F32).astype(BF16)
        high = weights_ref[...].astype(BF16)
        low = (weights_ref[...] - high.astype(F32)).astype(BF16)
        lane = lax.broadcasted_iota(jnp.int32, (top, 128), 1)
        row = lax.broadcasted_iota(jnp.int32, (top, 128), 0)
        facts = jnp.zeros((n, 128), F32)
        for at, part in enumerate((named, high, low)):
            place = jnp.where(lane == row + at * top, 1.0, 0.0).astype(BF16)
            facts = facts + jnp.dot(part, place, preferred_element_type=F32)
        out_ref[:, width:] = facts.astype(BF16)

    return pl.pallas_call(
        kernel, out_shape=jax.ShapeDtypeStruct((n, width + 128), BF16), name="with_facts"
    )(tokens, ids, weights)


def front(odd, rows, gates, ups):
    count, width = rows.shape
    units, block = gates[0].shape[1], 1024
    steps = width // block

    def kernel(odd_ref, rows_ref, gate_own, gate_other, up_own, up_other, out_ref, total):
        k = pl.program_id(0)

        @pl.when(k == 0)
        def _():
            total[...] = jnp.zeros_like(total)

        weights = jnp.concatenate([gate_own[...], gate_other[...], up_own[...], up_other[...]], 1)
        total[...] += jnp.dot(rows_ref[...], weights, preferred_element_type=F32)

        @pl.when(k == steps - 1)
        def _():
            gate, up = total[:, :2 * units], total[:, 2 * units:]
            hidden = gate / (1.0 + jnp.exp(-gate)) * up
            low, high = hidden[:, :units], hidden[:, units:]
            swap = odd_ref[0] == 1
            first, second = jnp.where(swap, high, low).astype(BF16), jnp.where(swap, low, high).astype(BF16)
            for at in range(4):
                out_ref[at, :, :units] = first
                out_ref[at, :, units:] = second

    weight = pl.BlockSpec((block, units), lambda k: (k, 0))
    return pl.pallas_call(
        kernel,
        grid=(steps,),
        in_specs=[
            pl.BlockSpec(memory_space=pltpu.SMEM),
            pl.BlockSpec((count, block), lambda k: (0, k)),
            weight, weight, weight, weight,
        ],
        out_specs=whole((4, count, 2 * units)),
        out_shape=jax.ShapeDtypeStruct((4, count, 2 * units), BF16),
        scratch_shapes=[pltpu.VMEM((count, 4 * units), F32)],
        name="front",
    )(odd, rows, *gates, *ups)


def back(odd, hidden, own, other, slots):
    parts, count, units = hidden.shape
    features = own.shape[1]
    steps = parts // 2

    def kernel(odd_ref, hidden_ref, own_ref, other_ref, out_ref, total):
        k = pl.program_id(0)

        @pl.when(k == 0)
        def _():
            total[...] = jnp.zeros_like(total)

        rows = jnp.concatenate([hidden_ref[0], hidden_ref[1]], 1)
        weights = jnp.concatenate([own_ref[...], other_ref[...]], 1)
        total[...] += jnp.dot(rows, weights, preferred_element_type=F32)

        @pl.when(k == steps - 1)
        def _():
            low, high = total[:, :features], total[:, features:]
            swap = odd_ref[0] == 1
            shape = (count // slots, slots, features)
            out_ref[:, :, :features] = jnp.where(swap, high, low).astype(BF16).reshape(shape)
            out_ref[:, :, features:] = jnp.where(swap, low, high).astype(BF16).reshape(shape)

    weight = pl.BlockSpec((2 * units, features), lambda k: (k, 0))
    out = (count // slots, slots, 2 * features)
    return pl.pallas_call(
        kernel,
        grid=(steps,),
        in_specs=[
            pl.BlockSpec(memory_space=pltpu.SMEM),
            pl.BlockSpec((2, count, units), lambda k: (k, 0, 0)),
            weight, weight,
        ],
        out_specs=whole(out),
        out_shape=jax.ShapeDtypeStruct(out, BF16),
        scratch_shapes=[pltpu.VMEM((count, 2 * features), F32)],
        name="back",
    )(odd, hidden, own, other)


def shards(tokens, expert_ids, gate_weights, w_gate, w_up, w_down, norm_gain):
    n, width = tokens.shape
    top = expert_ids.shape[1]
    g = lax.axis_index("grp")
    p = lax.axis_index("ep")
    odd = (g % 2).astype(jnp.int32).reshape(1)

    gate_own, up_own, down_own = w_gate[0], w_up[0], w_down[0]
    gate_other, up_other, down_other = pair_swap(gate_own), pair_swap(up_own), pair_swap(down_own)

    column = gather_column(with_facts(tokens, expert_ids, gate_weights))
    column, gate_other = lax.optimization_barrier((column, gate_other))
    parts = column, core_swap(column)
    half = parts[0].shape[0]
    rows = 2 * half
    slots = rows // 4

    take = (jnp.arange(3 * top)[:, None] == jnp.arange(128)[None, :]).astype(BF16)
    facts = [
        lax.dot_general(take, part[:, width:], (((1,), (1,)), ((), ())), preferred_element_type=F32)
        for part in parts
    ]
    facts = jnp.concatenate(facts, 1).reshape(3, top, rows)

    experts = (2 * p + jnp.arange(2)).astype(F32)
    match = facts[0][None] == experts[:, None, None]
    hit = jnp.any(match, axis=1)
    before = jnp.arange(rows)[:, None] < jnp.arange(rows)[None, :]
    place = jnp.dot(hit.astype(BF16), before.astype(BF16), preferred_element_type=F32)
    place = jnp.where(hit, place, -1.0)
    picks = place[:, None, :] == jnp.arange(slots, dtype=F32)[None, :, None]
    picks = picks.reshape(2 * slots, rows)
    onehot = picks.astype(BF16)
    chosen = jnp.dot(onehot[:, :half], parts[0][:, :width], preferred_element_type=F32)
    chosen = chosen + jnp.dot(onehot[:, half:], parts[1][:, :width], preferred_element_type=F32)
    chosen = chosen.astype(BF16).reshape(2, 1, slots, width)
    fanned = jnp.broadcast_to(chosen, (2, 4, slots, width)).reshape(8, slots, width)

    arrived = lax.all_to_all(fanned, "grp", split_axis=0, concat_axis=0, tiled=True, axis_index_groups=EIGHTS)
    arrived = arrived.reshape(8 * slots, width)

    hidden = front(odd, arrived, (gate_own, gate_other), (up_own, up_other))
    hidden, down_other = lax.optimization_barrier((hidden, down_other))
    hidden = lax.all_to_all(hidden, "grp", split_axis=0, concat_axis=0, tiled=True, axis_index_groups=FOURS)

    out = back(odd, hidden, down_own, down_other, slots)
    home = lax.all_to_all(out, "grp", split_axis=0, concat_axis=0, tiled=True, axis_index_groups=EIGHTS)
    half_width = home.shape[2] // 2
    home = jnp.concatenate(
        [
            jnp.concatenate(
                [home[of + j, :, half_width * at:half_width * (at + 1)] for j in range(4) for at in range(2)], 1
            )
            for of in (0, 4)
        ],
        0,
    )

    def weight(at):
        summed = jnp.sum(jnp.where(match, facts[at][None], 0.0), axis=1)
        summed = jnp.broadcast_to(summed[:, None], (2, slots, rows)).reshape(2 * slots, rows)
        return jnp.where(picks, summed, 0.0).astype(BF16)

    table = jnp.concatenate([weight(1), weight(2)], 0)
    home = jnp.concatenate([home, home], 0)

    def weighted(at):
        return lax.dot_general(at, home, (((0,), (0,)), ((), ())), preferred_element_type=F32)

    swapped = core_swap(weighted(table[:, half:]).astype(BF16))
    column = weighted(table[:, :half]) + swapped.astype(F32)
    mixed = tokens.astype(F32) + scatter_group(column, n)
    factor = lax.rsqrt(jnp.mean(mixed * mixed, axis=1, keepdims=True) + 1e-06)
    return (mixed * factor * norm_gain).astype(BF16)


def solution(mesh):
    placed = (
        P(("grp", "ep"), None),
        P(("grp", "ep"), None),
        P(("grp", "ep"), None),
        P("ep", None, "grp"),
        P("ep", None, "grp"),
        P("ep", None, "grp"),
        P(),
    )
    return jax.shard_map(
        shards, mesh=mesh, in_specs=placed, out_specs=P(("grp", "ep"), None), check_vma=False
    )
```

```python
import jax
import jax.numpy as jnp
from jax import lax
from jax.experimental import pallas as pl
from jax.experimental.pallas import tpu as pltpu
from jax.sharding import PartitionSpec as P

BF16 = jnp.bfloat16
F32 = jnp.float32


def around(block, chips):
    size = lax.axis_size("ep")
    return lax.ppermute(block, "ep", [(i, (i + 2 * chips) % size) for i in range(size)])


def core_swap(block):
    return lax.ppermute(block, "ep", [(i, i ^ 1) for i in range(lax.axis_size("ep"))])


def pair_swap(block):
    return lax.ppermute(block, "grp", [(i, i ^ 1) for i in range(lax.axis_size("grp"))])


EIGHTS = [[4 * y + x for y in range(4) for x in pair] for pair in ((0, 3), (1, 2))]
FOURS = [group[at:at + 4] for group in EIGHTS for at in (0, 4)]


def gather_column(block):
    n = block.shape[0]
    three = jnp.concatenate([block, around(block, 5), around(block, -5)], 0)
    below1, above1 = around(three, 1), around(three, -1)
    eighth = around(three[2 * n:], -3)
    below2, above2 = around(below1, 1), around(above1, -1)
    return jnp.concatenate([three, below1, above1, below2, above2, eighth], 0)


def scatter_group(column, n):
    sent = column[3 * n:].astype(BF16)
    below1, above1, below2, above2 = (sent[3 * n * i:3 * n * (i + 1)] for i in range(4))
    from_above2, from_below2 = around(below2, -2), around(above2, 2)
    eighth = around(sent[12 * n:], 3)
    from_above1, from_below1 = around(below1, -1), around(above1, 1)
    part = column[:3 * n]
    for other in (from_above2, from_below2, from_above1, from_below1):
        part = part + other.astype(F32)
    below = around(part[n:2 * n].astype(BF16), -5)
    above = around((part[2 * n:] + eighth.astype(F32)).astype(BF16), 5)
    return part[:n] + below.astype(F32) + above.astype(F32)


def whole(shape):
    return pl.BlockSpec(shape, lambda k: (0,) * len(shape))


def with_facts(tokens, ids, weights):
    n, width = tokens.shape
    top = ids.shape[1]

    def kernel(tokens_ref, ids_ref, weights_ref, out_ref):
        out_ref[:, :width] = tokens_ref[...]
        named = ids_ref[...].astype(F32).astype(BF16)
        high = weights_ref[...].astype(BF16)
        low = (weights_ref[...] - high.astype(F32)).astype(BF16)
        lane = lax.broadcasted_iota(jnp.int32, (top, 128), 1)
        row = lax.broadcasted_iota(jnp.int32, (top, 128), 0)
        facts = jnp.zeros((n, 128), F32)
        for at, part in enumerate((named, high, low)):
            place = jnp.where(lane == row + at * top, 1.0, 0.0).astype(BF16)
            facts = facts + jnp.dot(part, place, preferred_element_type=F32)
        out_ref[:, width:] = facts.astype(BF16)

    return pl.pallas_call(
        kernel, out_shape=jax.ShapeDtypeStruct((n, width + 128), BF16), name="with_facts"
    )(tokens, ids, weights)


def front(odd, rows, gates, ups):
    count, width = rows.shape
    units, block = gates[0].shape[1], 2048
    steps = width // block

    def kernel(odd_ref, rows_ref, gate_own, gate_other, up_own, up_other, out_ref, total):
        k = pl.program_id(0)

        @pl.when(k == 0)
        def _():
            total[...] = jnp.zeros_like(total)

        weights = jnp.concatenate([gate_own[...], gate_other[...], up_own[...], up_other[...]], 1)
        total[...] += jnp.dot(rows_ref[...], weights, preferred_element_type=F32)

        @pl.when(k == steps - 1)
        def _():
            gate, up = total[:, :2 * units], total[:, 2 * units:]
            hidden = gate / (1.0 + jnp.exp(-gate)) * up
            low, high = hidden[:, :units], hidden[:, units:]
            swap = odd_ref[0] == 1
            first, second = jnp.where(swap, high, low).astype(BF16), jnp.where(swap, low, high).astype(BF16)
            for at in range(4):
                out_ref[at, :, :units] = first
                out_ref[at, :, units:] = second

    weight = pl.BlockSpec((block, units), lambda k: (k, 0))
    return pl.pallas_call(
        kernel,
        grid=(steps,),
        in_specs=[
            pl.BlockSpec(memory_space=pltpu.SMEM),
            pl.BlockSpec((count, block), lambda k: (0, k)),
            weight, weight, weight, weight,
        ],
        out_specs=whole((4, count, 2 * units)),
        out_shape=jax.ShapeDtypeStruct((4, count, 2 * units), BF16),
        scratch_shapes=[pltpu.VMEM((count, 4 * units), F32)],
        compiler_params=pltpu.CompilerParams(vmem_limit_bytes=32 * 2**20),
        name="front",
    )(odd, rows, *gates, *ups)


def back(odd, hidden, own, other, slots):
    parts, count, units = hidden.shape
    features = own.shape[1]
    steps = parts // 2

    def kernel(odd_ref, hidden_ref, own_ref, other_ref, out_ref, total):
        k = pl.program_id(0)

        @pl.when(k == 0)
        def _():
            total[...] = jnp.zeros_like(total)

        rows = jnp.concatenate([hidden_ref[0], hidden_ref[1]], 1)
        weights = jnp.concatenate([own_ref[...], other_ref[...]], 1)
        total[...] += jnp.dot(rows, weights, preferred_element_type=F32)

        @pl.when(k == steps - 1)
        def _():
            low, high = total[:, :features], total[:, features:]
            swap = odd_ref[0] == 1
            shape = (count // slots, slots, features)
            out_ref[:, :, :features] = jnp.where(swap, high, low).astype(BF16).reshape(shape)
            out_ref[:, :, features:] = jnp.where(swap, low, high).astype(BF16).reshape(shape)

    weight = pl.BlockSpec((2 * units, features), lambda k: (k, 0))
    out = (count // slots, slots, 2 * features)
    return pl.pallas_call(
        kernel,
        grid=(steps,),
        in_specs=[
            pl.BlockSpec(memory_space=pltpu.SMEM),
            pl.BlockSpec((2, count, units), lambda k: (k, 0, 0)),
            weight, weight,
        ],
        out_specs=whole(out),
        out_shape=jax.ShapeDtypeStruct(out, BF16),
        scratch_shapes=[pltpu.VMEM((count, 2 * features), F32)],
        name="back",
    )(odd, hidden, own, other)


def shards(tokens, expert_ids, gate_weights, w_gate, w_up, w_down, norm_gain):
    n, width = tokens.shape
    top = expert_ids.shape[1]
    g = lax.axis_index("grp")
    p = lax.axis_index("ep")
    odd = (g % 2).astype(jnp.int32).reshape(1)

    gate_own, up_own, down_own = w_gate[0], w_up[0], w_down[0]
    gate_other, up_other = pair_swap(gate_own), pair_swap(up_own)

    column = gather_column(with_facts(tokens, expert_ids, gate_weights))
    parts = column, core_swap(column)
    half = parts[0].shape[0]
    rows = 2 * half
    slots = rows // 4

    take = (jnp.arange(3 * top)[:, None] == jnp.arange(128)[None, :]).astype(BF16)
    facts = [
        lax.dot_general(take, part[:, width:], (((1,), (1,)), ((), ())), preferred_element_type=F32)
        for part in parts
    ]
    facts = jnp.concatenate(facts, 1).reshape(3, top, rows)

    experts = (2 * p + jnp.arange(2)).astype(F32)
    match = facts[0][None] == experts[:, None, None]
    hit = jnp.any(match, axis=1)
    before = jnp.arange(rows)[:, None] < jnp.arange(rows)[None, :]
    place = jnp.dot(hit.astype(BF16), before.astype(BF16), preferred_element_type=F32)
    place = jnp.where(hit, place, -1.0)
    picks = place[:, None, :] == jnp.arange(slots, dtype=F32)[None, :, None]
    picks = picks.reshape(2 * slots, rows)
    onehot = picks.astype(BF16)
    chosen = jnp.dot(onehot[:, :half], parts[0][:, :width], preferred_element_type=F32)
    chosen = chosen + jnp.dot(onehot[:, half:], parts[1][:, :width], preferred_element_type=F32)
    chosen = chosen.astype(BF16).reshape(2, 1, slots, width)
    fanned = jnp.broadcast_to(chosen, (2, 4, slots, width)).reshape(8, slots, width)

    arrived = lax.all_to_all(fanned, "grp", split_axis=0, concat_axis=0, tiled=True, axis_index_groups=EIGHTS)
    arrived, down_own = lax.optimization_barrier((arrived, down_own))
    down_other = pair_swap(down_own)
    arrived = arrived.reshape(8 * slots, width)

    hidden = front(odd, arrived, (gate_own, gate_other), (up_own, up_other))
    hidden = lax.all_to_all(hidden, "grp", split_axis=0, concat_axis=0, tiled=True, axis_index_groups=FOURS)

    out = back(odd, hidden, down_own, down_other, slots)
    home = lax.all_to_all(out, "grp", split_axis=0, concat_axis=0, tiled=True, axis_index_groups=EIGHTS)
    half_width = home.shape[2] // 2
    home = jnp.concatenate(
        [
            jnp.concatenate(
                [home[of + j, :, half_width * at:half_width * (at + 1)] for j in range(4) for at in range(2)], 1
            )
            for of in (0, 4)
        ],
        0,
    )

    def weight(at):
        summed = jnp.sum(jnp.where(match, facts[at][None], 0.0), axis=1)
        summed = jnp.broadcast_to(summed[:, None], (2, slots, rows)).reshape(2 * slots, rows)
        return jnp.where(picks, summed, 0.0).astype(BF16)

    table = jnp.concatenate([weight(1), weight(2)], 0)
    home = jnp.concatenate([home, home], 0)

    def weighted(at):
        return lax.dot_general(at, home, (((0,), (0,)), ((), ())), preferred_element_type=F32)

    swapped = core_swap(weighted(table[:, half:]).astype(BF16))
    column = weighted(table[:, :half]) + swapped.astype(F32)
    mixed = tokens.astype(F32) + scatter_group(column, n)
    factor = lax.rsqrt(jnp.mean(mixed * mixed, axis=1, keepdims=True) + 1e-06)
    return (mixed * factor * norm_gain).astype(BF16)


def solution(mesh):
    placed = (
        P(("grp", "ep"), None),
        P(("grp", "ep"), None),
        P(("grp", "ep"), None),
        P("ep", None, "grp"),
        P("ep", None, "grp"),
        P("ep", None, "grp"),
        P(),
    )
    return jax.shard_map(
        shards, mesh=mesh, in_specs=placed, out_specs=P(("grp", "ep"), None), check_vma=False
    )
```

```python
import jax
import jax.numpy as jnp
from jax import lax
from jax.experimental import pallas as pl
from jax.experimental.pallas import tpu as pltpu
from jax.sharding import PartitionSpec as P

BF16 = jnp.bfloat16
F32 = jnp.float32


def around(block, chips):
    size = lax.axis_size("ep")
    return lax.ppermute(block, "ep", [(i, (i + 2 * chips) % size) for i in range(size)])


def core_swap(block):
    return lax.ppermute(block, "ep", [(i, i ^ 1) for i in range(lax.axis_size("ep"))])


def pair_swap(block):
    return lax.ppermute(block, "grp", [(i, i ^ 1) for i in range(lax.axis_size("grp"))])


EIGHTS = [[4 * y + x for y in range(4) for x in pair] for pair in ((0, 3), (1, 2))]
FOURS = [group[at:at + 4] for group in EIGHTS for at in (0, 4)]


def gather_column(block):
    n = block.shape[0]
    three = jnp.concatenate([block, around(block, 5), around(block, -5)], 0)
    below1, above1 = around(three, 1), around(three, -1)
    eighth = around(three[2 * n:], -3)
    below2, above2 = around(below1, 1), around(above1, -1)
    return jnp.concatenate([three, below1, above1, below2, above2, eighth], 0)


def scatter_group(column, n):
    sent = column[3 * n:].astype(BF16)
    below1, above1, below2, above2 = (sent[3 * n * i:3 * n * (i + 1)] for i in range(4))
    from_above2, from_below2 = around(below2, -2), around(above2, 2)
    eighth = around(sent[12 * n:], 3)
    from_above1, from_below1 = around(below1, -1), around(above1, 1)
    part = column[:3 * n]
    for other in (from_above2, from_below2, from_above1, from_below1):
        part = part + other.astype(F32)
    below = around(part[n:2 * n].astype(BF16), -5)
    above = around((part[2 * n:] + eighth.astype(F32)).astype(BF16), 5)
    return part[:n] + below.astype(F32) + above.astype(F32)


def whole(shape):
    return pl.BlockSpec(shape, lambda k: (0,) * len(shape))


def with_facts(tokens, ids, weights):
    n, width = tokens.shape
    top = ids.shape[1]

    def kernel(tokens_ref, ids_ref, weights_ref, out_ref):
        out_ref[:, :width] = tokens_ref[...]
        named = ids_ref[...].astype(F32).astype(BF16)
        high = weights_ref[...].astype(BF16)
        low = (weights_ref[...] - high.astype(F32)).astype(BF16)
        lane = lax.broadcasted_iota(jnp.int32, (top, 128), 1)
        row = lax.broadcasted_iota(jnp.int32, (top, 128), 0)
        facts = jnp.zeros((n, 128), F32)
        for at, part in enumerate((named, high, low)):
            place = jnp.where(lane == row + at * top, 1.0, 0.0).astype(BF16)
            facts = facts + jnp.dot(part, place, preferred_element_type=F32)
        out_ref[:, width:] = facts.astype(BF16)

    return pl.pallas_call(
        kernel, out_shape=jax.ShapeDtypeStruct((n, width + 128), BF16), name="with_facts"
    )(tokens, ids, weights)


def front(odd, rows, gates, ups):
    count, width = rows.shape
    units, block = gates[0].shape[1], 2048
    steps = width // block

    def kernel(odd_ref, rows_ref, gate_own, gate_other, up_own, up_other, out_ref, total):
        k = pl.program_id(0)

        @pl.when(k == 0)
        def _():
            total[...] = jnp.zeros_like(total)

        weights = jnp.concatenate([gate_own[...], gate_other[...], up_own[...], up_other[...]], 1)
        total[...] += jnp.dot(rows_ref[...], weights, preferred_element_type=F32)

        @pl.when(k == steps - 1)
        def _():
            gate, up = total[:, :2 * units], total[:, 2 * units:]
            hidden = gate / (1.0 + jnp.exp(-gate)) * up
            low, high = hidden[:, :units], hidden[:, units:]
            swap = odd_ref[0] == 1
            first, second = jnp.where(swap, high, low).astype(BF16), jnp.where(swap, low, high).astype(BF16)
            for at in range(4):
                out_ref[at, :, :units] = first
                out_ref[at, :, units:] = second

    weight = pl.BlockSpec((block, units), lambda k: (k, 0))
    return pl.pallas_call(
        kernel,
        grid=(steps,),
        in_specs=[
            pl.BlockSpec(memory_space=pltpu.SMEM),
            pl.BlockSpec((count, block), lambda k: (0, k)),
            weight, weight, weight, weight,
        ],
        out_specs=whole((4, count, 2 * units)),
        out_shape=jax.ShapeDtypeStruct((4, count, 2 * units), BF16),
        scratch_shapes=[pltpu.VMEM((count, 4 * units), F32)],
        compiler_params=pltpu.CompilerParams(vmem_limit_bytes=32 * 2**20),
        name="front",
    )(odd, rows, *gates, *ups)


def back(odd, hidden, own, other, slots):
    parts, count, units = hidden.shape
    features = own.shape[1]
    steps = parts // 2

    def kernel(odd_ref, hidden_ref, own_ref, other_ref, out_ref, total):
        k = pl.program_id(0)

        @pl.when(k == 0)
        def _():
            total[...] = jnp.zeros_like(total)

        rows = jnp.concatenate([hidden_ref[0], hidden_ref[1]], 1)
        weights = jnp.concatenate([own_ref[...], other_ref[...]], 1)
        total[...] += jnp.dot(rows, weights, preferred_element_type=F32)

        @pl.when(k == steps - 1)
        def _():
            low, high = total[:, :features], total[:, features:]
            swap = odd_ref[0] == 1
            shape = (count // slots, slots, features)
            out_ref[:, :, :features] = jnp.where(swap, high, low).astype(BF16).reshape(shape)
            out_ref[:, :, features:] = jnp.where(swap, low, high).astype(BF16).reshape(shape)

    weight = pl.BlockSpec((2 * units, features), lambda k: (k, 0))
    out = (count // slots, slots, 2 * features)
    return pl.pallas_call(
        kernel,
        grid=(steps,),
        in_specs=[
            pl.BlockSpec(memory_space=pltpu.SMEM),
            pl.BlockSpec((2, count, units), lambda k: (k, 0, 0)),
            weight, weight,
        ],
        out_specs=whole(out),
        out_shape=jax.ShapeDtypeStruct(out, BF16),
        scratch_shapes=[pltpu.VMEM((count, 2 * features), F32)],
        name="back",
    )(odd, hidden, own, other)


def shards(tokens, expert_ids, gate_weights, w_gate, w_up, w_down, norm_gain):
    n, width = tokens.shape
    top = expert_ids.shape[1]
    g = lax.axis_index("grp")
    p = lax.axis_index("ep")
    odd = (g % 2).astype(jnp.int32).reshape(1)

    gate_own, up_own, down_own = w_gate[0], w_up[0], w_down[0]
    gate_other, up_other, down_other = pair_swap(gate_own), pair_swap(up_own), pair_swap(down_own)

    column = gather_column(with_facts(tokens, expert_ids, gate_weights))
    column, gate_other = lax.optimization_barrier((column, gate_other))
    parts = column, core_swap(column)
    half = parts[0].shape[0]
    rows = 2 * half
    slots = rows // 4

    take = (jnp.arange(3 * top)[:, None] == jnp.arange(128)[None, :]).astype(BF16)
    facts = [
        lax.dot_general(take, part[:, width:], (((1,), (1,)), ((), ())), preferred_element_type=F32)
        for part in parts
    ]
    facts = jnp.concatenate(facts, 1).reshape(3, top, rows)

    experts = (2 * p + jnp.arange(2)).astype(F32)
    match = facts[0][None] == experts[:, None, None]
    hit = jnp.any(match, axis=1)
    before = jnp.arange(rows)[:, None] < jnp.arange(rows)[None, :]
    place = jnp.dot(hit.astype(BF16), before.astype(BF16), preferred_element_type=F32)
    place = jnp.where(hit, place, -1.0)
    picks = place[:, None, :] == jnp.arange(slots, dtype=F32)[None, :, None]
    picks = picks.reshape(2 * slots, rows)
    onehot = picks.astype(BF16)
    chosen = jnp.dot(onehot[:, :half], parts[0][:, :width], preferred_element_type=F32)
    chosen = chosen + jnp.dot(onehot[:, half:], parts[1][:, :width], preferred_element_type=F32)
    chosen = chosen.astype(BF16).reshape(2, 1, slots, width)
    fanned = jnp.broadcast_to(chosen, (2, 4, slots, width)).reshape(8, slots, width)

    arrived = lax.all_to_all(fanned, "grp", split_axis=0, concat_axis=0, tiled=True, axis_index_groups=EIGHTS)
    arrived = arrived.reshape(8 * slots, width)

    hidden = front(odd, arrived, (gate_own, gate_other), (up_own, up_other))
    hidden, down_other = lax.optimization_barrier((hidden, down_other))
    hidden = lax.all_to_all(hidden, "grp", split_axis=0, concat_axis=0, tiled=True, axis_index_groups=FOURS)

    out = back(odd, hidden, down_own, down_other, slots)
    home = lax.all_to_all(out, "grp", split_axis=0, concat_axis=0, tiled=True, axis_index_groups=EIGHTS)
    half_width = home.shape[2] // 2
    home = jnp.concatenate(
        [
            jnp.concatenate(
                [home[of + j, :, half_width * at:half_width * (at + 1)] for j in range(4) for at in range(2)], 1
            )
            for of in (0, 4)
        ],
        0,
    )

    def weight(at):
        summed = jnp.sum(jnp.where(match, facts[at][None], 0.0), axis=1)
        summed = jnp.broadcast_to(summed[:, None], (2, slots, rows)).reshape(2 * slots, rows)
        return jnp.where(picks, summed, 0.0).astype(BF16)

    table = jnp.concatenate([weight(1), weight(2)], 0)
    home = jnp.concatenate([home, home], 0)

    def weighted(at):
        return lax.dot_general(at, home, (((0,), (0,)), ((), ())), preferred_element_type=F32)

    swapped = core_swap(weighted(table[:, half:]).astype(BF16))
    column = weighted(table[:, :half]) + swapped.astype(F32)
    mixed = tokens.astype(F32) + scatter_group(column, n)
    factor = lax.rsqrt(jnp.mean(mixed * mixed, axis=1, keepdims=True) + 1e-06)
    return (mixed * factor * norm_gain).astype(BF16)


def solution(mesh):
    placed = (
        P(("grp", "ep"), None),
        P(("grp", "ep"), None),
        P(("grp", "ep"), None),
        P("ep", None, "grp"),
        P("ep", None, "grp"),
        P("ep", None, "grp"),
        P(),
    )
    return jax.shard_map(
        shards, mesh=mesh, in_specs=placed, out_specs=P(("grp", "ep"), None), check_vma=False
    )
```
